32 devices in a mesh: view: 4 (over y, x), tile: 8 (over z, core).
Axes of the slice: x: 2, y: 2, z: 4, core: 2. Of those that a mesh axis runs over, the one named last changes fastest.
Arguments:
- latents: bfloat16 [16, 2048, 1536], P('view', 'tile'), may hold values from -14 to 14
- qkv_weight: bfloat16 [1536, 3072], replicated, may hold values from -0.15625 to 0.15625
- out_weight: bfloat16 [1024, 1536], replicated, may hold values from -0.1875 to 0.1875
- anchor: int32 [1], replicated, may hold values from 0 to 15
- epi_list: int32 [16, 16, 6], P('view'), may hold values from -1 to 31, as said below
Outputs:
- attn_out: bfloat16 [16, 2048, 1536], P('view', 'tile')
The draws below stay inside these ranges and needn't reach their ends.
Inputs may be any that keep to these rules, and one draw needn't show every extreme that they name: `epi_list`: row (v, b) lists distinct key blocks: an id c < 16 is block c of view (v - 1) mod 16, an id c >= 16 is block c - 16 of view (v + 1) mod 16; unused slots hold -1 and follow the used ones. Every row uses 1 to 6 slots, with a cap that varies from view to view, and some row uses all 6.
All inputs are finite; a program needn't handle non-finite values.
Results may differ from the reference program's by a relative error of at most 0.005.
The reference program's roundings to bfloat16 on the way (of `projected`, `joined`, `weights` and `attended`) count: a program that leaves them out, or rounds other values in their place, can miss the bound.
Values may be sent and summed in bfloat16 or wider, within the bound.
A program may use at most 128 MiB of HBM per device.

```python
import math
import jax
import jax.numpy as jnp
from jax import lax

D = 1536
HEADS = 8
HD = 128
VIEWS = 16
VT = 2048
BLK = 128
EMAX = 6
NBLK = 16


def draw_latents(key, part):
    key_one = jax.random.fold_in(key, 0)
    values = jax.random.normal(key_one, (VIEWS, VT, D), jnp.float32)
    return jnp.clip(values, -14.0, 14.0).astype(jnp.bfloat16)


def draw_epi_list(key, part):
    key_order, key_room, key_count, key_full = jax.random.split(key, 4)
    candidates = 2 * NBLK
    ranking = jax.random.randint(key_order, (VIEWS, NBLK, candidates), 0, 1 << 20) * candidates + jnp.arange(candidates, dtype=jnp.int32)
    chosen = jnp.argsort(ranking, axis=-1)[..., :EMAX].astype(jnp.int32)
    room = jax.random.randint(key_room, (VIEWS, 1), 1, EMAX + 1)
    counts = 1 + jax.random.randint(key_count, (VIEWS, NBLK), 0, room)
    fullest = jax.random.randint(key_full, (), 0, VIEWS)
    view_ids = jnp.arange(VIEWS, dtype=jnp.int32)[:, None]
    block_ids = jnp.arange(NBLK, dtype=jnp.int32)[None, :]
    counts = jnp.where((view_ids == fullest) & (block_ids == 0), EMAX, counts)
    slots = jnp.arange(EMAX, dtype=jnp.int32)
    return jnp.where(slots[None, None, :] < counts[..., None], chosen, -1).astype(jnp.int32)


def centred(stream_key, shape, deviation, limit, kind=jnp.bfloat16):
    result = deviation * jax.random.normal(stream_key, shape, jnp.float32)
    return jnp.clip(result, min=-limit, max=limit).astype(kind)


def setup_inputs(seed: int = 0) -> dict:
    streams_of = jax.random.split(jax.random.key(seed), 6)
    return {
        "latents": draw_latents(jax.random.fold_in(streams_of[5], 71), 0),
        "qkv_weight": centred(streams_of[1], (D, HEADS * 3 * HD), D ** -0.5, 0.15625),
        "out_weight": centred(streams_of[2], (HEADS * HD, D), (HEADS * HD) ** -0.5, 0.1875),
        "anchor": jax.random.randint(streams_of[3], (1,), 0, VIEWS).astype(jnp.int32),
        "epi_list": draw_epi_list(jax.random.fold_in(streams_of[5], 71), 0),
    }


def allowed_tokens(epi_rows):
    blocks = jnp.any(epi_rows[:, :, None] == jnp.arange(2 * NBLK, dtype=jnp.int32)[None, None, :], axis=1)
    nearby = jnp.repeat(jnp.repeat(blocks, BLK, axis=0), BLK, axis=1)
    always = jnp.ones((VT, VT), dtype=bool)
    return jnp.concatenate([always, nearby, always], axis=1)

def attend(queries, keys_part, values_part, allowed):
    scores = jnp.einsum('qd,kd->qk', queries.astype(jnp.float32), keys_part.astype(jnp.float32)) / math.sqrt(HD)
    scores = jnp.where(allowed, scores, -jnp.inf)
    row_peak = lax.optimization_barrier(jnp.max(scores, axis=1, keepdims=True))
    raised = jnp.exp(scores - row_peak)
    row_total = lax.optimization_barrier(jnp.sum(raised, axis=1, keepdims=True))
    weights = raised.astype(jnp.bfloat16)
    summed = jnp.einsum('qk,kd->qd', weights.astype(jnp.float32), values_part.astype(jnp.float32))
    return (summed / row_total).astype(jnp.bfloat16)

def reference(latents, qkv_weight, out_weight, anchor, epi_list):
    shaped = qkv_weight.reshape(D, HEADS, 3 * HD).astype(jnp.float32)

    def project(tokens):
        return jnp.einsum('td,dhc->htc', tokens.astype(jnp.float32), shaped).astype(jnp.bfloat16)
    projected = lax.map(project, latents)
    key_values = projected[..., HD:]
    anchored = lax.dynamic_index_in_dim(key_values, anchor[0].astype(jnp.int32), 0, keepdims=False)
    mixing = out_weight.reshape(HEADS, HD, D).astype(jnp.float32)

    def one_view(view_id):
        earlier = lax.dynamic_index_in_dim(key_values, ((view_id - 1) % VIEWS).astype(jnp.int32), 0, keepdims=False)
        following = lax.dynamic_index_in_dim(key_values, ((view_id + 1) % VIEWS).astype(jnp.int32), 0, keepdims=False)
        resident = lax.dynamic_index_in_dim(projected, view_id, 0, keepdims=False)
        joined = jnp.concatenate([resident[..., HD:], earlier, following, anchored], axis=1)
        allowed = allowed_tokens(lax.dynamic_index_in_dim(epi_list, view_id, 0, keepdims=False))

        def one_head(head_items):
            queries, keyvals = head_items
            return attend(queries, keyvals[:, :HD], keyvals[:, HD:], allowed)
        attended = lax.map(one_head, (resident[..., :HD], joined))
        return jnp.einsum('htc,hcd->td', attended.astype(jnp.float32), mixing).astype(jnp.bfloat16)
    return lax.map(one_view, jnp.arange(VIEWS, dtype=jnp.int32))
```

```python
import functools
import math

import jax
import jax.numpy as jnp
from jax import lax
from jax.experimental import pallas as pl
from jax.experimental.pallas import tpu as pltpu
from jax.sharding import PartitionSpec as P

HEADS = 8
HD = 128
BLK = 128
LOG_SCALE = math.log2(math.e) / math.sqrt(HD)
NT = (((1,), (1,)), ((), ()))


def attention_kernel(rows, chunk, epi_ref, q_ref, own_ref, earlier_ref, following_ref, anchor_ref,
                     out_ref, keys, values):
    tokens = own_ref.shape[0]
    slots = epi_ref.shape[1]
    step = pl.program_id(0)

    @pl.when(step == 0)
    def _():
        for part, (ref, first) in enumerate(
            ((own_ref, HD), (anchor_ref, 0), (earlier_ref, 0), (following_ref, 0))
        ):
            span = pl.ds(part * tokens, tokens)
            keys[span, :] = ref[:, first:first + HD]
            values[span, :HD] = ref[:, first + HD:first + 2 * HD]
            values[span, HD:] = jnp.ones((tokens, HD), values.dtype)

    queries = q_ref[:, :HD]

    def scores_of(query_rows, key_rows):
        return lax.dot_general(query_rows, key_rows, NT, preferred_element_type=jnp.float32)

    def fold(state, scores, value_rows):
        peak = jnp.max(scores, axis=1, keepdims=True) * LOG_SCALE
        if state is not None:
            peak = jnp.maximum(state[0], peak)
        weights = jnp.exp2(scores * LOG_SCALE - peak).astype(jnp.bfloat16)
        summed = jnp.dot(weights, value_rows, preferred_element_type=jnp.float32)
        if state is not None:
            summed = summed + state[1] * jnp.exp2(state[0] - peak)
        return peak, summed

    state = None
    for start in range(0, 2 * tokens, chunk):
        state = fold(state, scores_of(queries, keys[start:start + chunk, :]),
                     values[start:start + chunk, :])

    per_step = rows // BLK
    for sub in range(per_step):
        block = step * per_step + sub
        span = slice(sub * BLK, (sub + 1) * BLK)
        key_rows, value_rows, used = [], [], []
        for slot in range(slots):
            entry = epi_ref[block, slot]
            place = pl.multiple_of(2 * tokens + jnp.maximum(entry, 0) * BLK, BLK)
            key_rows.append(keys[pl.ds(place, BLK), :])
            value_rows.append(values[pl.ds(place, BLK), :])
            used.append(entry >= 0)
        scores = scores_of(queries[span], jnp.concatenate(key_rows, axis=0))
        scores = jnp.concatenate(
            [
                jnp.where(used[slot], scores[:, slot * BLK:(slot + 1) * BLK], -jnp.inf)
                for slot in range(slots)
            ],
            axis=1,
        )
        _, summed = fold((state[0][span], state[1][span]), scores,
                         jnp.concatenate(value_rows, axis=0))
        out_ref[span, :] = (summed[:, :HD] / summed[:, HD:]).astype(out_ref.dtype)


def attend(epi_rows, queries, own, earlier, following, anchored, rows=512, chunk=1024):
    tokens = own.shape[0]
    count = queries.shape[0]
    rows = min(rows, count)
    chunk = min(chunk, tokens)
    whole = lambda array: pl.BlockSpec(array.shape, lambda i: (0, 0))
    return pl.pallas_call(
        functools.partial(attention_kernel, rows, chunk),
        grid=(count // rows,),
        in_specs=[
            pl.BlockSpec(memory_space=pltpu.SMEM),
            pl.BlockSpec((rows, queries.shape[1]), lambda i: (i, 0)),
            whole(own), whole(earlier), whole(following), whole(anchored),
        ],
        out_specs=pl.BlockSpec((rows, HD), lambda i: (i, 0)),
        out_shape=jax.ShapeDtypeStruct((count, HD), jnp.bfloat16),
        scratch_shapes=[
            pltpu.VMEM((4 * tokens, HD), jnp.bfloat16),
            pltpu.VMEM((4 * tokens, 2 * HD), jnp.bfloat16),
        ],
        compiler_params=pltpu.CompilerParams(vmem_limit_bytes=48 * 1024 * 1024),
        cost_estimate=pl.CostEstimate(
            flops=4 * count * 3 * tokens * HD * 2,
            bytes_accessed=2 * HD * (9 * tokens + 2 * count),
            transcendentals=count * 3 * tokens,
        ),
    )(epi_rows, queries, own, earlier, following, anchored)


def spread_2(array, axis, root):
    mine = lax.axis_index(axis) == root
    return lax.psum(jnp.where(mine, array, jnp.zeros_like(array)), axis)


def from_behind(array, axis, by):
    count = lax.axis_size(axis)
    return lax.ppermute(array, axis, [(i, (i + by) % count) for i in range(count)])


def body(latents, qkv_weight, out_weight, anchor, epi_list):
    per_dev, tile_tokens, model_width = latents.shape
    tile_count = lax.axis_size("tile")
    view_tokens = tile_tokens * tile_count
    parts = tile_count // HEADS
    part_rows = view_tokens // parts
    shaped = qkv_weight.reshape(model_width, HEADS, 3 * HD)
    tile_index = lax.axis_index("tile")

    resident = []
    for view in range(per_dev):
        projected = jnp.einsum(
            "td,dhc->htc", latents[view], shaped, preferred_element_type=jnp.float32
        ).astype(jnp.bfloat16)
        wide = jnp.broadcast_to(projected[:, None], (HEADS, parts, tile_tokens, 3 * HD))
        received = lax.all_to_all(
            wide.reshape(tile_count, tile_tokens, 3 * HD), "tile",
            split_axis=0, concat_axis=0, tiled=True,
        )
        resident.append(received.reshape(view_tokens, 3 * HD))

    key_values = [array[:, HD:] for array in resident]
    target = anchor[0]
    anchored = key_values[0]
    for view in range(1, per_dev):
        anchored = jnp.where(target % per_dev == view, key_values[view], anchored)
    anchored = spread_2(anchored, "view", target // per_dev)
    before = from_behind(key_values[per_dev - 1], "view", 1)
    after = from_behind(key_values[0], "view", -1)
    around = [before] + key_values + [after]

    own_part = tile_index % parts
    outs = []
    for view in range(per_dev):
        queries = resident[view]
        if parts > 1:
            queries = lax.dynamic_slice_in_dim(queries, own_part * part_rows, part_rows, 0)
        epi_rows = epi_list[view]
        if parts > 1:
            blocks = part_rows // BLK
            epi_rows = lax.dynamic_slice_in_dim(epi_rows, own_part * blocks, blocks, 0)
        attended = attend(epi_rows, queries, resident[view], around[view], around[view + 2],
                          anchored)
        outgoing = attended.reshape(1, tile_count // parts, tile_tokens, HD)
        if parts > 1:
            mine = jnp.arange(parts, dtype=jnp.int32)[:, None, None, None] == own_part
            outgoing = jnp.where(mine, outgoing, jnp.zeros((), jnp.bfloat16))
        returned = lax.all_to_all(
            outgoing.reshape(tile_count, tile_tokens, HD), "tile",
            split_axis=0, concat_axis=0, tiled=True,
        ).reshape(HEADS, parts, tile_tokens, HD)
        home = tile_index // (tile_count // parts)
        returned = lax.dynamic_index_in_dim(returned, home, 1, keepdims=False)
        outs.append(
            jnp.einsum(
                "htc,hcd->td", returned, out_weight.reshape(HEADS, HD, model_width),
                preferred_element_type=jnp.float32,
            ).astype(jnp.bfloat16)
        )
    return jnp.stack(outs)


def solution(mesh):
    return jax.shard_map(
        body,
        mesh=mesh,
        in_specs=(P("view", "tile", None), P(), P(), P(), P("view", None, None)),
        out_specs=P("view", "tile", None),
        check_vma=False,
    )
```

```python
import functools
import math

import jax
import jax.numpy as jnp
import numpy as np
from jax import lax
from jax.experimental import pallas as pl
from jax.experimental.pallas import tpu as pltpu
from jax.sharding import PartitionSpec as P

HEADS = 8
HD = 128
BLK = 128
LOG_SCALE = math.log2(math.e) / math.sqrt(HD)
NT = (((1,), (1,)), ((), ()))


def spread_2(array, axis, root):
    mine = lax.axis_index(axis) == root
    return lax.psum(jnp.where(mine, array, jnp.zeros_like(array)), axis)


def from_behind(array, axis, by):
    count = lax.axis_size(axis)
    return lax.ppermute(array, axis, [(i, (i + by) % count) for i in range(count)])


def project_kernel(view_ref, tokens_ref, weight_ref, out_ref):
    out_ref[0] = jnp.dot(
        tokens_ref[0], weight_ref[...], preferred_element_type=jnp.float32
    ).astype(out_ref.dtype)


def project(view, latents, weight):
    _, tokens, width = latents.shape
    return pl.pallas_call(
        project_kernel,
        grid_spec=pltpu.PrefetchScalarGridSpec(
            num_scalar_prefetch=1,
            grid=(HEADS,),
            in_specs=[
                pl.BlockSpec((1, tokens, width), lambda h, view: (view[0], 0, 0)),
                pl.BlockSpec((width, 3 * HD), lambda h, view: (0, h)),
            ],
            out_specs=pl.BlockSpec((1, tokens, 3 * HD), lambda h, view: (h, 0, 0)),
        ),
        out_shape=jax.ShapeDtypeStruct((HEADS, tokens, 3 * HD), jnp.bfloat16),
        compiler_params=pltpu.CompilerParams(vmem_limit_bytes=24 * 1024 * 1024),
        cost_estimate=pl.CostEstimate(
            flops=2 * tokens * width * HEADS * 3 * HD,
            bytes_accessed=2 * HEADS * 3 * HD * (width + tokens),
            transcendentals=0,
        ),
    )(view.reshape(1), latents, weight)


def scores_of(query_rows, key_rows):
    return lax.dot_general(query_rows, key_rows, NT, preferred_element_type=jnp.float32)


def fold(state, scores, value_rows):
    peak = jnp.max(scores, axis=1, keepdims=True) * LOG_SCALE
    if state is not None:
        peak = jnp.maximum(state[0], peak)
    weights = jnp.exp2(scores * LOG_SCALE - peak).astype(jnp.bfloat16)
    summed = jnp.dot(weights, value_rows, preferred_element_type=jnp.float32)
    if state is not None:
        summed = summed + state[1] * jnp.exp2(state[0] - peak)
    return peak, summed


def dense_kernel(chunk, q_ref, own_k, own_v, anchor_k, anchor_v, sum_ref, stat_ref, values):
    tokens = own_k.shape[0]

    @pl.when(pl.program_id(0) == 0)
    def _():
        values[:tokens, :HD] = own_v[...]
        values[tokens:, :HD] = anchor_v[...]
        values[:, HD:] = jnp.ones((2 * tokens, HD), values.dtype)

    queries = q_ref[...]
    state = None
    for part, key_ref in enumerate((own_k, anchor_k)):
        for start in range(0, tokens, chunk):
            first = part * tokens + start
            state = fold(state, scores_of(queries, key_ref[start:start + chunk, :]),
                         values[first:first + chunk, :])
    peak, summed = state
    sum_ref[...] = summed[:, :HD]
    lane = lax.broadcasted_iota(jnp.int32, stat_ref.shape, 1)
    stat_ref[...] = jnp.where(lane < HD // 2, summed[:, HD:], peak)


def dense(queries, own, anchored, rows=512, chunk=1024):
    tokens = own.shape[0]
    count = queries.shape[0]
    rows = min(rows, count)
    chunk = min(chunk, tokens)
    column = lambda c: pl.BlockSpec((tokens, HD), lambda i: (0, c))
    by_rows = pl.BlockSpec((rows, HD), lambda i: (i, 0))
    return pl.pallas_call(
        functools.partial(dense_kernel, chunk),
        grid=(count // rows,),
        in_specs=[by_rows, column(1), column(2), column(0), column(1)],
        out_specs=[by_rows, by_rows],
        out_shape=[jax.ShapeDtypeStruct((count, HD), jnp.float32)] * 2,
        scratch_shapes=[pltpu.VMEM((2 * tokens, 2 * HD), jnp.bfloat16)],
        compiler_params=pltpu.CompilerParams(vmem_limit_bytes=40 * 1024 * 1024),
        cost_estimate=pl.CostEstimate(
            flops=8 * count * 2 * tokens * HD,
            bytes_accessed=8 * HD * tokens + 10 * HD * count,
            transcendentals=count * 2 * tokens,
        ),
    )(queries, own, own, anchored, anchored)


def nearby_kernel(local, pick_ref, epi_ref, q_ref, sum_ref, stat_ref, *refs):
    sources, (out_ref, near, sems) = refs[:-3], refs[-3:]
    tokens = near.shape[0] // 2
    rows = q_ref.shape[0]
    slots = epi_ref.shape[1]
    step = pl.program_id(0)

    @pl.when(step == 0)
    def _():
        for side in range(2):
            for index, source in enumerate(sources):
                first = HD if index < local else 0

                @pl.when(pick_ref[side] == index)
                def _():
                    pltpu.make_async_copy(
                        source.at[:, pl.ds(first, 2 * HD)],
                        near.at[pl.ds(side * tokens, tokens), :], sems.at[side],
                    ).start()
        for side in range(2):
            pltpu.make_async_copy(
                sources[-1], near.at[pl.ds(side * tokens, tokens), :], sems.at[side]
            ).wait()

    per_step = rows // BLK
    ones = jnp.ones((BLK, HD), near.dtype)
    for sub in range(per_step):
        block = step * per_step + sub
        span = slice(sub * BLK, (sub + 1) * BLK)
        key_rows, value_rows, used = [], [], []
        for slot in range(slots):
            entry = epi_ref[block, slot]
            place = pl.multiple_of(jnp.maximum(entry, 0) * BLK, BLK)
            key_rows.append(near[pl.ds(place, BLK), :HD])
            value_rows.append(
                jnp.concatenate([near[pl.ds(place, BLK), HD:], ones], axis=1)
            )
            used.append(entry >= 0)
        scores = scores_of(q_ref[span, :], jnp.concatenate(key_rows, axis=0))
        scores = jnp.concatenate(
            [
                jnp.where(used[slot], scores[:, slot * BLK:(slot + 1) * BLK], -jnp.inf)
                for slot in range(slots)
            ],
            axis=1,
        )
        peak = stat_ref[span, HD // 2:HD // 2 + 1]
        total = jnp.broadcast_to(stat_ref[span, 0:1], (BLK, HD))
        state = (peak, jnp.concatenate([sum_ref[span, :], total], axis=1))
        _, summed = fold(state, scores, jnp.concatenate(value_rows, axis=0))
        out_ref[span, :] = (summed[:, :HD] / summed[:, HD:]).astype(out_ref.dtype)


def nearby(picks, epi_rows, queries, sums, stats, sources, rows=512):
    count = queries.shape[0]
    tokens = sources[0].shape[0]
    rows = min(rows, count)
    by_rows = pl.BlockSpec((rows, HD), lambda i: (i, 0))
    slots = epi_rows.shape[1]
    return pl.pallas_call(
        functools.partial(nearby_kernel, len(sources) - 2),
        grid=(count // rows,),
        in_specs=[pl.BlockSpec(memory_space=pltpu.SMEM)] * 2 + [by_rows] * 3
        + [pl.BlockSpec(memory_space=pl.ANY)] * len(sources),
        out_specs=by_rows,
        out_shape=jax.ShapeDtypeStruct((count, HD), jnp.bfloat16),
        scratch_shapes=[
            pltpu.VMEM((2 * tokens, 2 * HD), jnp.bfloat16),
            pltpu.SemaphoreType.DMA((2,)),
        ],
        compiler_params=pltpu.CompilerParams(vmem_limit_bytes=24 * 1024 * 1024),
        cost_estimate=pl.CostEstimate(
            flops=8 * count * slots * BLK * HD,
            bytes_accessed=8 * HD * tokens + 12 * HD * count,
            transcendentals=count * slots * BLK,
        ),
    )(picks, epi_rows, queries, sums, stats, *sources)


def order_table(count):
    table = []
    for first in range(count):
        order = [first]
        for view in [0, count - 1] + list(range(count)):
            if view not in order:
                order.append(view)
        table.append(order)
    return np.array(table, np.int32)


def body(latents, qkv_weight, out_weight, anchor, epi_list):
    per_dev, tile_tokens, model_width = latents.shape
    tile_count = lax.axis_size("tile")
    view_tokens = tile_tokens * tile_count
    parts = tile_count // HEADS
    part_rows = view_tokens // parts
    tile_index = lax.axis_index("tile")
    own_part = tile_index % parts
    target = anchor[0]

    table = order_table(per_dev)
    order = jnp.asarray(table)[target % per_dev]
    where_is = jnp.asarray(np.argsort(table, axis=1).astype(np.int32))[target % per_dev]

    def chosen(arrays, index):
        result = arrays[0]
        for place in range(1, len(arrays)):
            result = jnp.where(index == place, arrays[place], result)
        return result

    resident = []
    for slot in range(per_dev):
        projected = project(order[slot], latents, qkv_weight)
        wide = jnp.broadcast_to(projected[:, None], (HEADS, parts, tile_tokens, 3 * HD))
        wide = wide.reshape(tile_count, tile_tokens, 3 * HD)
        if resident:
            wide, resident[-1] = lax.optimization_barrier((wide, resident[-1]))
        received = lax.all_to_all(wide, "tile", split_axis=0, concat_axis=0, tiled=True)
        resident.append(received.reshape(view_tokens, 3 * HD))

    anchored = spread_2(resident[0][:, HD:], "view", target // per_dev)
    edge = min(3, per_dev)
    key_values = [array[:, HD:] for array in resident[:edge]]
    before = from_behind(chosen(key_values, where_is[per_dev - 1]), "view", 1)
    after = from_behind(chosen(key_values, where_is[0]), "view", -1)
    sources = resident + [before, after]

    out = jnp.zeros(latents.shape, jnp.bfloat16)
    home = tile_index // (tile_count // parts)
    for slot in range(per_dev):
        view = order[slot]
        queries = resident[slot]
        epi_rows = lax.dynamic_index_in_dim(epi_list, view, 0, keepdims=False)
        if parts > 1:
            blocks = part_rows // BLK
            queries = lax.dynamic_slice_in_dim(queries, own_part * part_rows, part_rows, 0)
            epi_rows = lax.dynamic_slice_in_dim(epi_rows, own_part * blocks, blocks, 0)
        sums, stats = dense(queries, resident[slot], anchored)
        earlier = jnp.where(view == 0, per_dev, where_is[jnp.maximum(view - 1, 0)])
        following = jnp.where(
            view == per_dev - 1, per_dev + 1, where_is[jnp.minimum(view + 1, per_dev - 1)]
        )
        picks = jnp.stack([earlier, following]).astype(jnp.int32)
        attended = nearby(picks, epi_rows, queries, sums, stats, sources)
        outgoing = attended.reshape(1, tile_count // parts, tile_tokens, HD)
        if parts > 1:
            mine = jnp.arange(parts, dtype=jnp.int32)[:, None, None, None] == own_part
            outgoing = jnp.where(mine, outgoing, jnp.zeros((), jnp.bfloat16))
        returned = lax.all_to_all(
            outgoing.reshape(tile_count, tile_tokens, HD), "tile",
            split_axis=0, concat_axis=0, tiled=True,
        ).reshape(HEADS, parts, tile_tokens, HD)
        returned = lax.dynamic_index_in_dim(returned, home, 1, keepdims=False)
        result = jnp.einsum(
            "htc,hcd->td", returned, out_weight.reshape(HEADS, HD, model_width),
            preferred_element_type=jnp.float32,
        ).astype(jnp.bfloat16)
        out = lax.dynamic_update_index_in_dim(out, result, view, 0)
    return out


def solution(mesh):
    return jax.shard_map(
        body,
        mesh=mesh,
        in_specs=(P("view", "tile", None), P(), P(), P(), P("view", None, None)),
        out_specs=P("view", "tile", None),
        check_vma=False,
    )
```
